128 devices in a mesh: grp: 8 (over z, core), ep: 16 (over y, x).
Axes of the slice: x: 4, y: 4, z: 4, core: 2. Of those that a mesh axis runs over, the one named last changes fastest.
Arguments:
- tokens: bfloat16 [16384, 6144], P(('grp', 'ep')), may hold values from -6 to 6
- routed_slots: int32 [7168], P(('grp', 'ep')), may hold values from -1 to 127, as said below
- combine_weight: float32 [7168], P(('grp', 'ep')), may hold values from 0.1 to 1
- gate_weight: bfloat16 [6144, 8192], P('grp', 'ep'), may hold values from -0.078125 to 0.078125
- up_weight: bfloat16 [6144, 8192], P('grp', 'ep'), may hold values from -0.078125 to 0.078125
- down_weight: bfloat16 [8192, 6144], P('ep', 'grp'), may hold values from -0.0625 to 0.0625
Outputs:
- mixed: bfloat16 [16384, 6144], P(('grp', 'ep'))
The draws below stay inside these ranges and needn't reach their ends.
Inputs may be any that keep to these rules, and one draw needn't show every extreme that they name: `routed_slots`: each owner's 56 slots hold distinct local token numbers, live ones in the first slots and -1 after them; in every draw all 16 owners of one replica have all 56 slots live.
All inputs are finite; a program needn't handle non-finite values.
Results may differ from the reference program's by a relative error of at most 0.019.
Values may be sent and summed in bfloat16 or wider, within the bound.
No kernel may reach another device: no remote copies, remote signals or barrier semaphores. Data moves between devices by JAX's collectives and lax.ppermute only.
A program may use at most 128 MiB of HBM per device.

```python
import jax
import jax.numpy as jnp
from jax import lax

D = 6144
FF = 8192
TOK_DEV = 128
CAP = 56
TOKENS = 16384
SLOTS = 7168
N_GRP = 8
N_EP = 16


def draw_routed_slots(key, part):
    key = jax.random.fold_in(key, 11)
    blocks = N_GRP * N_EP
    key_count, key_full, key_perm = jax.random.split(key, 3)
    counts = jax.random.randint(key_count, (N_GRP, N_EP), CAP // 4, CAP + 1)
    full_replica = jax.random.randint(key_full, (), 0, N_GRP)
    replica_ids = jnp.arange(N_GRP, dtype=jnp.int32)[:, None]
    counts = jnp.where(replica_ids == full_replica, CAP, counts).reshape(blocks)
    orders = jax.vmap(lambda sub_key: jax.random.permutation(sub_key, TOK_DEV)[:CAP])(jax.random.split(key_perm, blocks))
    positions = jnp.arange(CAP, dtype=jnp.int32)[None, :]
    chosen = jnp.where(positions < counts[:, None], orders, -1)
    return chosen.reshape(blocks * CAP).astype(jnp.int32)


def block_scale(rng, dims, cuts, least, top_value):
    def one(position, shards_of):
        steps = jax.random.uniform(jax.random.fold_in(jax.random.fold_in(rng, 6), position), (shards_of,), jnp.float32, least / len(cuts), top_value / len(cuts))
        return jnp.repeat(jnp.exp(steps), dims[position] // shards_of).reshape((-1,) + (1,) * (len(dims) - position - 1))

    level = one(*cuts[0])
    for cut in cuts[1:]:
        level = level * one(*cut)
    return level


def bell_draw(own_key, extent, deviation, most, shards=(), kind=jnp.bfloat16):
    factor_of = block_scale(own_key, extent, shards, -0.22, 0.18) if shards else 1.0
    result = jax.random.normal(own_key, extent, jnp.float32) * deviation * factor_of
    return jnp.minimum(jnp.maximum(result, -most), most).astype(kind)


def setup_inputs(seed: int = 0) -> dict:
    key_of = jax.random.split(jax.random.key(seed), 7)
    return {
        "tokens": bell_draw(key_of[0], (TOKENS, D), 1.0, 6.0, ((0, 128),)),
        "routed_slots": draw_routed_slots(jax.random.fold_in(key_of[6], 71), 0),
        "combine_weight": jnp.clip(0.1 + 0.9 * jax.random.uniform(key_of[2], (SLOTS,), jnp.float32) ** block_scale(key_of[2], (SLOTS,), ((0, 128),), -0.2, 0.2), 0.1, 1.0),
        "gate_weight": bell_draw(key_of[3], (D, FF), D ** -0.5, 0.078125, ((0, 8), (1, 16))),
        "up_weight": bell_draw(key_of[4], (D, FF), D ** -0.5, 0.078125, ((0, 8), (1, 16))),
        "down_weight": bell_draw(key_of[5], (FF, D), FF ** -0.5, 0.0625, ((0, 16), (1, 8))),
    }


def expert_rows(rows, gate_weight, up_weight, down_weight):
    gate_sum = jnp.dot(rows, gate_weight, preferred_element_type=jnp.float32)
    up_sum = jnp.dot(rows, up_weight, preferred_element_type=jnp.float32)
    hidden = (jax.nn.silu(gate_sum) * up_sum).astype(jnp.bfloat16)
    block_width = FF // N_EP
    total = jnp.zeros((rows.shape[0], D), jnp.float32)
    for block in range(N_EP):
        lower = block * block_width
        partial_value = jnp.dot(hidden[:, lower:lower + block_width], down_weight[lower:lower + block_width], preferred_element_type=jnp.float32)
        rounded = lax.optimization_barrier(partial_value.astype(jnp.bfloat16))
        total = total + rounded.astype(jnp.float32)
    return total


def reference(tokens, routed_slots, combine_weight, gate_weight, up_weight, down_weight):
    blocks = N_GRP * N_EP
    slot_table = routed_slots.reshape(blocks, CAP)
    offsets = (jnp.arange(blocks, dtype=jnp.int32) * TOK_DEV)[:, None]
    valid = (slot_table >= 0).reshape(-1)
    index = jnp.where(slot_table >= 0, slot_table + offsets, 0).reshape(-1).astype(jnp.int32)
    packed = jnp.where(valid[:, None], tokens[index], jnp.zeros((), jnp.bfloat16)).astype(jnp.bfloat16)
    grouped = packed.reshape(N_GRP, N_EP * CAP, D)
    expert_out = lax.map(lambda rows: expert_rows(rows, gate_weight, up_weight, down_weight), grouped)
    expert_out = expert_out.reshape(blocks * CAP, D)
    weighted = expert_out * combine_weight[:, None]
    target = jnp.where(valid, index, blocks * TOK_DEV).astype(jnp.int32)
    mixed = jnp.zeros((blocks * TOK_DEV, D), jnp.float32).at[target].add(weighted, mode="drop")
    return mixed.astype(jnp.bfloat16)
```

```python
import jax
import jax.numpy as jnp
from jax import lax
from jax.experimental import pallas as pl
from jax.experimental.pallas import tpu as pltpu
from jax.sharding import PartitionSpec as P

BOTH = ("grp", "ep")
F32, BF16 = jnp.float32, jnp.bfloat16


def first(core):
    return 1 if core == 0 else 3


def pairs(axis, step):
    out = []
    for g in range(8):
        z, c = divmod(g, 2)
        off = first(c) if step == 0 else 4 - first(c)
        for e in range(16):
            y, x = divmod(e, 4)
            x2 = x ^ off if axis == "x" else x
            y2 = y ^ off if axis == "y" else y
            z2 = z ^ off if axis == "z" else z
            out.append((g * 16 + e, (2 * z2 + c) * 16 + 4 * y2 + x2))
    return out


PAIRS = {axis: (pairs(axis, 0), pairs(axis, 1)) for axis in "xyz"}
SWAP = [(g * 16 + e, (g ^ 1) * 16 + e) for g in range(8) for e in range(16)]


def exchange(value, axis, step):
    return lax.ppermute(value, BOTH, PAIRS[axis][step])


def swap(value):
    return lax.ppermute(value, BOTH, SWAP)


def shard_order():
    table = []
    for g in range(8):
        z, c = divmod(g, 2)
        p = first(c)
        q = 4 - p
        own = [2 * (z ^ o) + c for o in (0, p, q, 2)]
        other = [2 * (z ^ o) + 1 - c for o in (0, q, p, 2)]
        table.append(own[:2] + other[:2] + own[2:] + other[2:])
    return table


def pack(order, routed_slots, tokens):
    cap, width = routed_slots.shape[0], tokens.shape[1] // 8

    def kernel(order_ref, slots_ref, tokens_ref, a_ref, b_ref):
        ids = lax.broadcasted_iota(jnp.int32, (tokens.shape[0], cap), 0)
        pick = (ids == slots_ref[...]).astype(F32).T.astype(BF16)
        for j in range(8):
            start = pl.multiple_of(order_ref[j] * width, 128)
            part = jnp.dot(pick, tokens_ref[:, pl.ds(start, width)], preferred_element_type=F32).astype(BF16)
            target = a_ref if j < 4 else b_ref
            target[:, (j % 4) * width : (j % 4 + 1) * width] = part

    return pl.pallas_call(
        kernel,
        in_specs=[pl.BlockSpec(memory_space=pltpu.SMEM), pl.BlockSpec(memory_space=pltpu.VMEM), pl.BlockSpec(memory_space=pltpu.VMEM)],
        out_specs=[pl.BlockSpec(memory_space=pltpu.VMEM)] * 2,
        out_shape=[jax.ShapeDtypeStruct((cap, 4 * width), BF16)] * 2,
        compiler_params=pltpu.CompilerParams(vmem_limit_bytes=16 * 2**20),
        name="pack",
    )(order, routed_slots.reshape(1, cap), tokens)


def place(order, routed_slots, combine, pieces, tokens_here):
    cap = routed_slots.shape[0]
    width = pieces[0][0].shape[1] // 2

    def kernel(order_ref, slots_ref, combine_ref, *refs):
        out_ref = refs[-1]
        ids = lax.broadcasted_iota(jnp.int32, (tokens_here, cap), 0)
        put = (ids == slots_ref[...]).astype(BF16)
        for k in range(4):
            total = refs[2 * k][...].astype(F32) + refs[2 * k + 1][...].astype(F32)
            value = (combine_ref[...] * total).astype(BF16)
            rows = jnp.dot(put, value, preferred_element_type=F32).astype(BF16)
            for i in range(2):
                start = pl.multiple_of(order_ref[2 * k + i] * width, 128)
                out_ref[:, pl.ds(start, width)] = rows[:, i * width : (i + 1) * width]

    flat = [v for pair in pieces for v in pair]
    return pl.pallas_call(
        kernel,
        in_specs=[pl.BlockSpec(memory_space=pltpu.SMEM)] + [pl.BlockSpec(memory_space=pltpu.VMEM)] * (2 + len(flat)),
        out_specs=pl.BlockSpec(memory_space=pltpu.VMEM),
        out_shape=jax.ShapeDtypeStruct((tokens_here, 8 * width), BF16),
        compiler_params=pltpu.CompilerParams(vmem_limit_bytes=16 * 2**20),
        name="place",
    )(order, routed_slots.reshape(1, cap), combine.reshape(cap, 1), *flat)


def gather_rows(own, axes):
    value = own
    for axis in axes:
        for step in (0, 1):
            got = exchange(value, axis, step)
            if axis == axes[1] and step == 1:
                return value, got
            value = jnp.concatenate([value, got], axis=0)


def dot(a, b):
    return jnp.dot(a, b, preferred_element_type=F32)


def sum_rows(near, far, axes):
    got = exchange(far, axes[0], 1)
    rest = near
    for axis, step in ((axes[0], 0), (axes[1], 1), (axes[1], 0)):
        total = rest + got.astype(F32)
        half = total.shape[0] // 2
        rest = total[:half]
        got = exchange(total[half:].astype(BF16), axis, step)
    return rest, got


def on_device(tokens, routed_slots, combine_weight, gate_weight, up_weight, down_weight):
    cap = routed_slots.shape[0]
    order = jnp.asarray(shard_order(), jnp.int32)[lax.axis_index("grp")]

    both = jnp.concatenate([gate_weight, up_weight], axis=1)
    near_w = jnp.concatenate([both, exchange(both, "z", 0)], axis=0)
    far_w = exchange(near_w, "z", 1)
    near_w2, far_w2 = swap(near_w), swap(far_w)

    own_a, own_b = pack(order, routed_slots, tokens)
    near_a, far_a = gather_rows(own_a, "xy")
    near_b, far_b = gather_rows(own_b, "yx")

    near_d = jnp.concatenate([down_weight, exchange(down_weight, "z", 0)], axis=1)
    far_d = exchange(near_d, "z", 1)
    near_d2, far_d2 = swap(near_d), swap(far_d)

    k = near_w.shape[0]

    def up_sums(rows, w, w2):
        return dot(rows[:, :k], w) + dot(rows[:, k:], w2)

    acc_a = jnp.concatenate([up_sums(near_a, near_w, near_w2), up_sums(far_a, near_w, near_w2)], axis=0)
    acc_b = jnp.concatenate([up_sums(near_b, far_w, far_w2), up_sums(far_b, far_w, far_w2)], axis=0)
    wide = acc_a.shape[1]

    def other_order(v):
        return v.reshape(4, 4, cap, -1).swapaxes(0, 1).reshape(16 * cap, -1)

    acc = acc_a + other_order(acc_b)
    ff = wide // 2
    hidden_a = (jax.nn.silu(acc[:, :ff]) * acc[:, ff:]).astype(BF16)
    hidden_b = other_order(hidden_a)

    half = 8 * cap
    pieces = []
    for w, w2 in ((near_d, near_d2), (far_d, far_d2)):
        for h, wd, axes in ((hidden_a, w, "yx"), (hidden_b, w2, "xy")):
            pieces.append(sum_rows(dot(h[:half], wd), dot(h[half:], wd).astype(BF16), axes))
    return place(order, routed_slots, combine_weight, pieces, tokens.shape[0])


def solution(mesh):
    placed = (
        P(("grp", "ep"), None),
        P(("grp", "ep")),
        P(("grp", "ep")),
        P("grp", "ep"),
        P("grp", "ep"),
        P("ep", "grp"),
    )
    return jax.shard_map(
        on_device, mesh=mesh, in_specs=placed, out_specs=P(("grp", "ep"), None), check_vma=False
    )
```

```python
import jax
import jax.numpy as jnp
from jax import lax
from jax.experimental import pallas as pl
from jax.experimental.pallas import tpu as pltpu
from jax.sharding import PartitionSpec as P

BOTH = ("grp", "ep")
F32, BF16 = jnp.float32, jnp.bfloat16


def pairs(kind, off):
    out = []
    for g in range(8):
        z, c = divmod(g, 2)
        for e in range(16):
            y, x = divmod(e, 4)
            place = {"x": x, "y": y, "z": z}
            axis = {"z": "z", "in": "xy"[c], "out": "yx"[c]}[kind]
            place[axis] ^= 4 - off if kind == "z" and c == 1 else off
            out.append((g * 16 + e, (2 * place["z"] + c) * 16 + 4 * place["y"] + place["x"]))
    return out


P_OFF, Q_OFF = 1, 3
PAIRS = {(kind, off): pairs(kind, off) for kind in ("z", "in", "out") for off in (P_OFF, Q_OFF)}
SWAP = [(g * 16 + e, (g ^ 1) * 16 + e) for g in range(8) for e in range(16)]


def exchange(value, kind, off):
    return lax.ppermute(value, BOTH, PAIRS[kind, off])


def swap(value):
    return lax.ppermute(value, BOTH, SWAP)


def shard_order():
    table = []
    for g in range(8):
        z, c = divmod(g, 2)
        p, q = (P_OFF, Q_OFF) if c == 0 else (Q_OFF, P_OFF)
        own = [2 * (z ^ o) + c for o in (0, p, q, 2)]
        other = [2 * (z ^ o) + 1 - c for o in (0, q, p, 2)]
        table.append(own[:2] + other[:2] + own[2:] + other[2:])
    return table


def pack(order, routed_slots, tokens):
    cap, width = routed_slots.shape[0], tokens.shape[1] // 8

    def kernel(order_ref, slots_ref, tokens_ref, a_ref, b_ref):
        ids = lax.broadcasted_iota(jnp.int32, (tokens.shape[0], cap), 0)
        pick = (ids == slots_ref[...]).astype(F32).T.astype(BF16)
        for j in range(8):
            start = pl.multiple_of(order_ref[j] * width, 128)
            part = jnp.dot(pick, tokens_ref[:, pl.ds(start, width)], preferred_element_type=F32).astype(BF16)
            target = a_ref if j < 4 else b_ref
            target[:, (j % 4) * width : (j % 4 + 1) * width] = part

    return pl.pallas_call(
        kernel,
        in_specs=[pl.BlockSpec(memory_space=pltpu.SMEM), pl.BlockSpec(memory_space=pltpu.VMEM), pl.BlockSpec(memory_space=pltpu.VMEM)],
        out_specs=[pl.BlockSpec(memory_space=pltpu.VMEM)] * 2,
        out_shape=[jax.ShapeDtypeStruct((cap, 4 * width), BF16)] * 2,
        compiler_params=pltpu.CompilerParams(vmem_limit_bytes=16 * 2**20),
        name="pack",
    )(order, routed_slots.reshape(1, cap), tokens)


def place(order, routed_slots, combine, pieces, tokens_here):
    cap = routed_slots.shape[0]
    width = pieces[0][0].shape[1] // 2

    def kernel(order_ref, slots_ref, combine_ref, *refs):
        out_ref = refs[-1]
        ids = lax.broadcasted_iota(jnp.int32, (tokens_here, cap), 0)
        put = (ids == slots_ref[...]).astype(BF16)
        for k in range(4):
            total = refs[2 * k][...].astype(F32) + refs[2 * k + 1][...].astype(F32)
            value = (combine_ref[...] * total).astype(BF16)
            rows = jnp.dot(put, value, preferred_element_type=F32).astype(BF16)
            for i in range(2):
                start = pl.multiple_of(order_ref[2 * k + i] * width, 128)
                out_ref[:, pl.ds(start, width)] = rows[:, i * width : (i + 1) * width]

    flat = [v for pair in pieces for v in pair]
    return pl.pallas_call(
        kernel,
        in_specs=[pl.BlockSpec(memory_space=pltpu.SMEM)] + [pl.BlockSpec(memory_space=pltpu.VMEM)] * (2 + len(flat)),
        out_specs=pl.BlockSpec(memory_space=pltpu.VMEM),
        out_shape=jax.ShapeDtypeStruct((tokens_here, 8 * width), BF16),
        compiler_params=pltpu.CompilerParams(vmem_limit_bytes=16 * 2**20),
        name="place",
    )(order, routed_slots.reshape(1, cap), combine.reshape(cap, 1), *flat)


def dot(a, b):
    return jnp.dot(a, b, preferred_element_type=F32)


def stack(*parts):
    return jnp.concatenate(parts, axis=0)


def together(*values):
    return lax.optimization_barrier(values)


def swap_parts(value, parts):
    rows = value.shape[0] // parts
    return stack(*(swap(value[i * rows : (i + 1) * rows]) for i in range(parts))) if parts > 1 else swap(value)


def on_device(tokens, routed_slots, combine_weight, gate_weight, up_weight, down_weight):
    order = jnp.asarray(shard_order(), jnp.int32)[lax.axis_index("grp")]
    cap, ff = routed_slots.shape[0], gate_weight.shape[1]
    group = 4 * cap
    p, q = P_OFF, Q_OFF

    own_a, own_b = pack(order, routed_slots, tokens)
    a_1 = stack(own_a, exchange(own_a, "in", p))
    b_1 = stack(own_b, exchange(own_b, "in", q))
    w_0 = jnp.concatenate([gate_weight, up_weight], axis=1)
    near_w = stack(w_0, exchange(w_0, "z", p))
    a_2, b_2 = exchange(a_1, "in", q), exchange(b_1, "in", p)
    a0 = stack(a_1, a_2)
    b0 = stack(own_b, b_2[:cap], b_1[cap:], b_2[cap:])

    ap, bq = exchange(a0, "out", p), exchange(b0, "out", q)
    near_a, near_b = stack(a0, ap), stack(b0, bq)
    far_a, far_b = exchange(near_a, "out", q), exchange(near_b, "out", p)
    far_w = exchange(near_w, "z", q)
    near_w2, far_w2 = swap_parts(near_w, 1), swap_parts(far_w, 1)
    near_d = jnp.concatenate([down_weight, exchange(down_weight, "z", p)], axis=1)
    far_d = exchange(near_d, "z", q)
    near_d2, far_d2 = swap_parts(near_d, 1), swap_parts(far_d, 1)

    k = near_w.shape[0]
    act = lambda acc: (jax.nn.silu(acc[:, :ff]) * acc[:, ff:]).astype(BF16)
    acc_near_a = dot(near_a[:, :k], near_w) + dot(near_a[:, k:], near_w2)
    acc_near_b = dot(near_b[:, :k], far_w)
    far_a, far_b, acc_near_a, acc_near_b = together(far_a, far_b, acc_near_a, acc_near_b)
    acc_near_b = acc_near_b + dot(near_b[:, k:], far_w2)
    acc_far_a = dot(far_a[:, :k], near_w) + dot(far_a[:, k:], near_w2)
    acc_far_b = dot(far_b[:, :k], far_w) + dot(far_b[:, k:], far_w2)
    h_q2 = act(acc_far_a + stack(acc_near_b[group:], acc_far_b[group:]))
    h_0p = act(acc_near_a + stack(acc_near_b[:group], acc_far_b[:group]))
    h_p2 = stack(h_0p[group:], h_q2[group:])
    h_0q = stack(h_0p[:group], h_q2[:group])


    pieces = []
    for wds in ((near_d, near_d2), (far_d, far_d2)):
        for stay, leave, wd, off in ((h_0p, h_q2, wds[0], q), (h_0q, h_p2, wds[1], p)):
            got = exchange(dot(leave, wd).astype(BF16), "out", off)
            total = dot(stay, wd) + got.astype(F32)
            got = exchange(total[group:].astype(BF16), "out", 4 - off)
            total = total[:group] + got.astype(F32)
            block = lambda i: total[i * cap : (i + 1) * cap]
            one, two = (block(1), block(2)) if off == p else (block(2), block(1))
            got = exchange(stack(one, block(3)).astype(BF16), "in", off).astype(F32)
            last = exchange((two + got[cap:]).astype(BF16), "in", 4 - off)
            pieces.append((block(0) + got[:cap], last))
    return place(order, routed_slots, combine_weight, pieces, tokens.shape[0])


def solution(mesh):
    placed = (
        P(("grp", "ep"), None),
        P(("grp", "ep")),
        P(("grp", "ep")),
        P("grp", "ep"),
        P("grp", "ep"),
        P("ep", "grp"),
    )
    return jax.shard_map(
        on_device, mesh=mesh, in_specs=placed, out_specs=P(("grp", "ep"), None), check_vma=False
    )
```

```python
import jax
import jax.numpy as jnp
from jax import lax
from jax.experimental import pallas as pl
from jax.experimental.pallas import tpu as pltpu
from jax.sharding import PartitionSpec as P

BOTH = ("grp", "ep")
F32, BF16 = jnp.float32, jnp.bfloat16


def pairs(kind, off):
    out = []
    for g in range(8):
        z, c = divmod(g, 2)
        for e in range(16):
            y, x = divmod(e, 4)
            place = {"x": x, "y": y, "z": z}
            axis = {"z": "z", "in": "xy"[c], "out": "yx"[c]}[kind]
            place[axis] ^= 4 - off if kind == "z" and c == 1 else off
            out.append((g * 16 + e, (2 * place["z"] + c) * 16 + 4 * place["y"] + place["x"]))
    return out


P_OFF, Q_OFF = 1, 3
PAIRS = {(kind, off): pairs(kind, off) for kind in ("z", "in", "out") for off in (P_OFF, Q_OFF)}
SWAP = [(g * 16 + e, (g ^ 1) * 16 + e) for g in range(8) for e in range(16)]


def exchange(value, kind, off):
    return lax.ppermute(value, BOTH, PAIRS[kind, off])


def swap(value):
    return lax.ppermute(value, BOTH, SWAP)


def shard_order():
    g = lax.axis_index("grp")
    z, c = g // 2, g % 2
    p = jnp.where(c == 0, P_OFF, Q_OFF)
    q = 4 - p
    own = [2 * (z ^ o) + c for o in (0, p, q, 2)]
    other = [2 * (z ^ o) + 1 - c for o in (0, q, p, 2)]
    return own[:2] + other[:2] + own[2:] + other[2:]


def pack(routed_slots, tokens):
    cap, width = routed_slots.shape[0], tokens.shape[1] // 8

    def kernel(slots_ref, tokens_ref, a_ref, b_ref):
        ids = lax.broadcasted_iota(jnp.int32, (tokens.shape[0], cap), 0)
        pick = (ids == slots_ref[...]).astype(F32).T.astype(BF16)
        order = shard_order()
        for j in range(8):
            start = pl.multiple_of(order[j] * width, 128)
            part = jnp.dot(pick, tokens_ref[:, pl.ds(start, width)], preferred_element_type=F32).astype(BF16)
            target = a_ref if j < 4 else b_ref
            target[:, (j % 4) * width : (j % 4 + 1) * width] = part

    return pl.pallas_call(
        kernel,
        in_specs=[pl.BlockSpec(memory_space=pltpu.VMEM), pl.BlockSpec(memory_space=pltpu.VMEM)],
        out_specs=[pl.BlockSpec(memory_space=pltpu.VMEM)] * 2,
        out_shape=[jax.ShapeDtypeStruct((cap, 4 * width), BF16)] * 2,
        compiler_params=pltpu.CompilerParams(vmem_limit_bytes=16 * 2**20),
        name="pack",
    )(routed_slots.reshape(1, cap), tokens)


def place(routed_slots, combine, pieces, tokens_here):
    cap = routed_slots.shape[0]
    width = pieces[0][0].shape[1] // 2

    def kernel(slots_ref, combine_ref, *refs):
        out_ref = refs[-1]
        order = shard_order()
        ids = lax.broadcasted_iota(jnp.int32, (tokens_here, cap), 0)
        put = (ids == slots_ref[...]).astype(BF16)
        for k in range(4):
            total = refs[2 * k][...].astype(F32) + refs[2 * k + 1][...].astype(F32)
            value = (combine_ref[...] * total).astype(BF16)
            rows = jnp.dot(put, value, preferred_element_type=F32).astype(BF16)
            for i in range(2):
                start = pl.multiple_of(order[2 * k + i] * width, 128)
                out_ref[:, pl.ds(start, width)] = rows[:, i * width : (i + 1) * width]

    flat = [v for pair in pieces for v in pair]
    return pl.pallas_call(
        kernel,
        in_specs=[pl.BlockSpec(memory_space=pltpu.VMEM)] * (2 + len(flat)),
        out_specs=pl.BlockSpec(memory_space=pltpu.VMEM),
        out_shape=jax.ShapeDtypeStruct((tokens_here, 8 * width), BF16),
        compiler_params=pltpu.CompilerParams(vmem_limit_bytes=16 * 2**20),
        name="place",
    )(routed_slots.reshape(1, cap), combine.reshape(cap, 1), *flat)


def dot(a, b):
    return jnp.dot(a, b, preferred_element_type=F32)


def stack(*parts):
    return jnp.concatenate(parts, axis=0)


def together(*values):
    return lax.optimization_barrier(values)


def swap_parts(value, parts):
    rows = value.shape[0] // parts
    return stack(*(swap(value[i * rows : (i + 1) * rows]) for i in range(parts))) if parts > 1 else swap(value)


def on_device(tokens, routed_slots, combine_weight, gate_weight, up_weight, down_weight):
    cap, ff = routed_slots.shape[0], gate_weight.shape[1]
    group = 4 * cap
    p, q = P_OFF, Q_OFF

    own_a, own_b = pack(routed_slots, tokens)
    a_1 = stack(own_a, exchange(own_a, "in", p))
    b_1 = stack(own_b, exchange(own_b, "in", q))
    w_0 = jnp.concatenate([gate_weight, up_weight], axis=1)
    near_w = stack(w_0, exchange(w_0, "z", p))
    a_2, b_2 = exchange(a_1, "in", q), exchange(b_1, "in", p)
    a0 = stack(a_1, a_2)
    b0 = stack(own_b, b_2[:cap], b_1[cap:], b_2[cap:])

    ap, bq = exchange(a0, "out", p), exchange(b0, "out", q)
    near_a, near_b = stack(a0, ap), stack(b0, bq)
    far_a, far_b = exchange(near_a, "out", q), exchange(near_b, "out", p)
    far_w = exchange(near_w, "z", q)
    near_w2, far_w2 = swap_parts(near_w, 1), swap_parts(far_w, 1)
    near_d = jnp.concatenate([down_weight, exchange(down_weight, "z", p)], axis=1)
    far_d = exchange(near_d, "z", q)
    near_d2, far_d2 = swap_parts(near_d, 1), swap_parts(far_d, 1)

    k = near_w.shape[0]
    act = lambda acc: (jax.nn.silu(acc[:, :ff]) * acc[:, ff:]).astype(BF16)
    acc_near_a = dot(near_a[:, :k], near_w) + dot(near_a[:, k:], near_w2)
    acc_near_b = dot(near_b[:, :k], far_w)
    far_a, far_b, acc_near_a, acc_near_b = together(far_a, far_b, acc_near_a, acc_near_b)
    acc_near_b = acc_near_b + dot(near_b[:, k:], far_w2)
    acc_far_a = dot(far_a[:, :k], near_w) + dot(far_a[:, k:], near_w2)
    acc_far_b = dot(far_b[:, :k], far_w) + dot(far_b[:, k:], far_w2)
    h_q2 = act(acc_far_a + stack(acc_near_b[group:], acc_far_b[group:]))
    h_0p = act(acc_near_a + stack(acc_near_b[:group], acc_far_b[:group]))
    h_p2 = stack(h_0p[group:], h_q2[group:])
    h_0q = stack(h_0p[:group], h_q2[:group])


    pieces = []
    for wds in ((near_d, near_d2), (far_d, far_d2)):
        for stay, leave, wd, off in ((h_0p, h_q2, wds[0], q), (h_0q, h_p2, wds[1], p)):
            got = exchange(dot(leave, wd).astype(BF16), "out", off)
            total = dot(stay, wd) + got.astype(F32)
            got = exchange(total[group:].astype(BF16), "out", 4 - off)
            total = total[:group] + got.astype(F32)
            block = lambda i: total[i * cap : (i + 1) * cap]
            one, two = (block(1), block(2)) if off == p else (block(2), block(1))
            got = exchange(stack(one, block(3)).astype(BF16), "in", off).astype(F32)
            last = exchange((two + got[cap:]).astype(BF16), "in", 4 - off)
            pieces.append((block(0) + got[:cap], last))
    return place(routed_slots, combine_weight, pieces, tokens.shape[0])


def solution(mesh):
    placed = (
        P(("grp", "ep"), None),
        P(("grp", "ep")),
        P(("grp", "ep")),
        P("grp", "ep"),
        P("grp", "ep"),
        P("ep", "grp"),
    )
    return jax.shard_map(
        on_device, mesh=mesh, in_specs=placed, out_specs=P(("grp", "ep"), None), check_vma=False
    )
```

```python
import jax
import jax.numpy as jnp
from jax import lax
from jax.experimental import pallas as pl
from jax.experimental.pallas import tpu as pltpu
from jax.sharding import PartitionSpec as P

BOTH = ("grp", "ep")
F32, BF16 = jnp.float32, jnp.bfloat16


def pairs(kind, off):
    out = []
    for g in range(8):
        z, c = divmod(g, 2)
        for e in range(16):
            y, x = divmod(e, 4)
            place = {"x": x, "y": y, "z": z}
            axis = {"z": "z", "in": "xy"[c], "out": "yx"[c]}[kind]
            place[axis] ^= 4 - off if kind == "z" and c == 1 else off
            out.append((g * 16 + e, (2 * place["z"] + c) * 16 + 4 * place["y"] + place["x"]))
    return out


P_OFF, Q_OFF = 1, 3
PAIRS = {(kind, off): pairs(kind, off) for kind in ("z", "in", "out") for off in (P_OFF, Q_OFF)}
SWAP = [(g * 16 + e, (g ^ 1) * 16 + e) for g in range(8) for e in range(16)]


def exchange(value, kind, off):
    return lax.ppermute(value, BOTH, PAIRS[kind, off])


def swap(value):
    return lax.ppermute(value, BOTH, SWAP)


def shard_order():
    g = lax.axis_index("grp")
    z, c = g // 2, g % 2
    p = jnp.where(c == 0, P_OFF, Q_OFF)
    q = 4 - p
    own = [2 * (z ^ o) + c for o in (0, p, q, 2)]
    other = [2 * (z ^ o) + 1 - c for o in (0, q, p, 2)]
    return own[:2] + other[:2] + own[2:] + other[2:]


def pack(routed_slots, tokens):
    cap, width = routed_slots.shape[0], tokens.shape[1] // 8

    def kernel(slots_ref, tokens_ref, a_ref, b_ref):
        ids = lax.broadcasted_iota(jnp.int32, (tokens.shape[0], cap), 0)
        pick = (ids == slots_ref[...]).astype(F32).T.astype(BF16)
        order = shard_order()
        for j in range(8):
            start = pl.multiple_of(order[j] * width, 128)
            part = jnp.dot(pick, tokens_ref[:, pl.ds(start, width)], preferred_element_type=F32).astype(BF16)
            target = a_ref if j < 4 else b_ref
            target[:, (j % 4) * width : (j % 4 + 1) * width] = part

    return pl.pallas_call(
        kernel,
        in_specs=[pl.BlockSpec(memory_space=pltpu.VMEM), pl.BlockSpec(memory_space=pltpu.VMEM)],
        out_specs=[pl.BlockSpec(memory_space=pltpu.VMEM)] * 2,
        out_shape=[jax.ShapeDtypeStruct((cap, 4 * width), BF16)] * 2,
        compiler_params=pltpu.CompilerParams(vmem_limit_bytes=16 * 2**20),
        name="pack",
    )(routed_slots.reshape(1, cap), tokens)


def place(routed_slots, combine, pieces, tokens_here, run, before=None):
    cap = routed_slots.shape[0]
    width = pieces[0][0].shape[1] // 2

    def kernel(slots_ref, combine_ref, *refs):
        out_ref, rows_ref, sems = refs[-3:]
        shards = shard_order()[4 * run : 4 * run + 4]
        ids = lax.broadcasted_iota(jnp.int32, (tokens_here, cap), 0)
        put = (ids == slots_ref[...]).astype(BF16)
        copies = []
        for k in range(2):
            total = refs[2 * k][...] + refs[2 * k + 1][...].astype(F32)
            value = (combine_ref[...] * total).astype(BF16)
            rows = jnp.dot(put, value, preferred_element_type=F32).astype(BF16)
            for i in range(2):
                j = 2 * k + i
                rows_ref[j] = rows[:, i * width : (i + 1) * width]
                start = pl.multiple_of(shards[j] * width, 128)
                copies.append(pltpu.make_async_copy(rows_ref.at[j], out_ref.at[:, pl.ds(start, width)], sems.at[j]))
                copies[j].start()
        for copy in copies:
            copy.wait()

    flat = [v for pair in pieces for v in pair]
    in_specs = [pl.BlockSpec(memory_space=pltpu.VMEM)] * (2 + len(flat))
    aliases = {}
    if before is not None:
        aliases = {len(in_specs): 0}
        in_specs, flat = in_specs + [pl.BlockSpec(memory_space=pl.ANY)], flat + [before]
    return pl.pallas_call(
        kernel,
        in_specs=in_specs,
        out_specs=pl.BlockSpec(memory_space=pl.ANY),
        out_shape=jax.ShapeDtypeStruct((tokens_here, 8 * width), BF16),
        input_output_aliases=aliases,
        scratch_shapes=[pltpu.VMEM((4, tokens_here, width), BF16), pltpu.SemaphoreType.DMA((4,))],
        compiler_params=pltpu.CompilerParams(vmem_limit_bytes=16 * 2**20),
        name="place",
    )(routed_slots.reshape(1, cap), combine.reshape(cap, 1), *flat)


def dot(a, b):
    return jnp.dot(a, b, preferred_element_type=F32)


def stack(*parts):
    return jnp.concatenate(parts, axis=0)


def together(*values):
    return lax.optimization_barrier(values)


def swap_parts(value, parts):
    rows = value.shape[0] // parts
    return stack(*(swap(value[i * rows : (i + 1) * rows]) for i in range(parts))) if parts > 1 else swap(value)


def on_device(tokens, routed_slots, combine_weight, gate_weight, up_weight, down_weight):
    cap, ff = routed_slots.shape[0], gate_weight.shape[1]
    group = 4 * cap
    p, q = P_OFF, Q_OFF

    w_0 = jnp.concatenate([gate_weight, up_weight], axis=1)
    near_w = stack(w_0, exchange(w_0, "z", p))
    own_a, own_b = pack(routed_slots, tokens)
    a_1 = stack(own_a, exchange(own_a, "in", p))
    b_1 = stack(own_b, exchange(own_b, "in", q))
    a_2, b_2 = exchange(a_1, "in", q), exchange(b_1, "in", p)
    a0 = stack(a_1, a_2)
    b0 = stack(own_b, b_2[:cap], b_1[cap:], b_2[cap:])

    ap, bq = exchange(a0, "out", p), exchange(b0, "out", q)
    near_a, near_b = stack(a0, ap), stack(b0, bq)
    far_a, far_b = exchange(near_a, "out", q), exchange(near_b, "out", p)
    far_w = exchange(near_w, "z", q)
    near_w2, far_w2 = swap_parts(near_w, 1), swap_parts(far_w, 1)
    near_d = jnp.concatenate([down_weight, exchange(down_weight, "z", p)], axis=1)
    far_d = exchange(near_d, "z", q)
    near_d2, far_d2 = swap_parts(near_d, 1), swap_parts(far_d, 1)

    k = near_w.shape[0]
    act = lambda acc: (jax.nn.silu(acc[:, :ff]) * acc[:, ff:]).astype(BF16)
    acc_near_a = dot(near_a[:, :k], near_w) + dot(near_a[:, k:], near_w2)
    acc_near_b = dot(near_b[:, :k], far_w)
    far_a, far_b, acc_near_a, acc_near_b = together(far_a, far_b, acc_near_a, acc_near_b)
    acc_near_b = acc_near_b + dot(near_b[:, k:], far_w2)
    acc_far_a = dot(far_a[:, :k], near_w) + dot(far_a[:, k:], near_w2)
    acc_far_b = dot(far_b[:, :k], far_w) + dot(far_b[:, k:], far_w2)
    h_q2 = act(acc_far_a + stack(acc_near_b[group:], acc_far_b[group:]))
    h_0p = act(acc_near_a + stack(acc_near_b[:group], acc_far_b[:group]))
    h_p2 = stack(h_0p[group:], h_q2[group:])
    h_0q = stack(h_0p[:group], h_q2[:group])


    pieces = []
    for wds in ((near_d, near_d2), (far_d, far_d2)):
        for stay, leave, wd, off in ((h_0p, h_q2, wds[0], q), (h_0q, h_p2, wds[1], p)):
            got = exchange(dot(leave, wd).astype(BF16), "out", off)
            total = dot(stay, wd) + got.astype(F32)
            got = exchange(total[group:].astype(BF16), "out", 4 - off)
            total = total[:group] + got.astype(F32)
            block = lambda i: total[i * cap : (i + 1) * cap]
            one, two = (block(1), block(2)) if off == p else (block(2), block(1))
            got = exchange(stack(one, block(3)).astype(BF16), "in", off).astype(F32)
            last = exchange((two + got[cap:]).astype(BF16), "in", 4 - off)
            pieces.append((block(0) + got[:cap], last))
    mixed = place(routed_slots, combine_weight, pieces[2:], tokens.shape[0], 1)
    return place(routed_slots, combine_weight, pieces[:2], tokens.shape[0], 0, mixed)


def solution(mesh):
    placed = (
        P(("grp", "ep"), None),
        P(("grp", "ep")),
        P(("grp", "ep")),
        P("grp", "ep"),
        P("grp", "ep"),
        P("ep", "grp"),
    )
    return jax.shard_map(
        on_device, mesh=mesh, in_specs=placed, out_specs=P(("grp", "ep"), None), check_vma=False
    )
```
